32 devices in a mesh: rep: 2 (over core), ep: 16 (over z, y, x).
Axes of the slice: x: 2, y: 2, z: 4, core: 2. Of those that a mesh axis runs over, the one named last changes fastest.
Arguments:
- resid_in: bfloat16 [2048, 2048], P(('rep', 'ep')), may hold values from -6 to 6
- context: bfloat16 [2048, 2048], P('rep', 'ep'), may hold values from -6 to 6
- out_proj: bfloat16 [2048, 2048], P('ep'), may hold values from -0.125 to 0.125
- norm_gain: float32 [2048], replicated, may hold values from 0.5 to 1.5
- router: bfloat16 [2048, 64], replicated, may hold values from -0.03125 to 0.03125
- routes: int32 [2048, 8], P(('rep', 'ep')), may hold values from 0 to 63, all different within a row; in each aligned block of 64 rows (0 to 63, 64 to 127, ...) at most 10 rows name the same one
- w_gate: bfloat16 [2048, 65536], P(None, ('rep', 'ep')), may hold values from -0.125 to 0.125
- w_up: bfloat16 [2048, 65536], P(None, ('rep', 'ep')), may hold values from -0.125 to 0.125
- w_down: bfloat16 [65536, 2048], P(('rep', 'ep')), may hold values from -0.5 to 0.5
- next_gain: float32 [2048], replicated, may hold values from 0.5 to 1.5
Outputs:
- resid_out: bfloat16 [2048, 2048], P(('rep', 'ep'))
- next_normed: bfloat16 [2048, 2048], P(('rep', 'ep'))
The draws below stay inside these ranges and needn't reach their ends.
Inputs may be any that keep to these rules, and one draw needn't show every extreme that they name: `routes`: each row names 8 different experts. Among the 64 rows of one device no expert is named by more than 10 rows, a bound that some block reaches.
All inputs are finite; a program needn't handle non-finite values.
Results may differ from the reference program's by a relative error of at most 0.014.
Values may be sent and summed in bfloat16 or wider, within the bound.
A program may use at most 192 MiB of HBM per device.

```python
import math
import jax
import jax.numpy as jnp
import numpy as np
from jax import lax

D = 2048
ATT = 2048
EXPERTS = 64
FF_E = 1024
TOP = 8
TOK_DEV = 64
MOST = 10
TOKENS = 2048
UNITS = 2048


def spiked(array, rng, source, target, blocks, factor):
    owner, partner = [(jnp.arange(array.shape[axis_at]) // (array.shape[axis_at] // blocks)).reshape([-1 if axis == axis_at else 1 for axis in range(array.ndim)]) for axis_at in (source, target)]
    chosen = jax.random.permutation(rng, blocks)[partner]
    strong = (owner == chosen) | (owner == (partner + blocks // 2) % blocks)
    return jnp.where(strong, factor * array, array)


def shard_levels(own_key, shape, split, low, high):
    level = 1.0
    for position, shards_of in split:
        heights = jax.random.uniform(jax.random.fold_in(jax.random.fold_in(own_key, 6), position), (shards_of,), jnp.float32, low / len(split), high / len(split))
        level = level * jnp.repeat(jnp.exp(heights), shape[position] // shards_of).reshape((-1,) + (1,) * (len(shape) - 1 - position))
    return level


def routed_block(stream_key, own, number, rows, amount, top, reach, lean):
    order = jax.random.permutation(stream_key, amount)
    heavy_load, common = shares(amount, rows * top, reach, lean, True), shares(amount, rows * top, reach, lean, False)
    places = jnp.arange(amount)

    def named(sizes, turn):
        used = int((sizes > 0).sum())
        fixed = max(1, used // 4)
        passed = fixed + (places - fixed + turn * (used - fixed)) % max(1, amount - fixed)
        return jnp.zeros((amount,), jnp.int32).at[order[jnp.where(places < fixed, places, passed)]].set(jnp.asarray(sizes, jnp.int32))

    sizes = jnp.where(number % 4 == 0, named(heavy_load, number // 4), named(common, number - number // 4 - 1))
    mixed = jax.random.permutation(jax.random.fold_in(own, 3), amount)
    giver, sink = mixed[0:amount // 2 * 2:2], mixed[1:amount // 2 * 2:2]
    room = jnp.minimum(sizes[giver] - 1, reach - sizes[sink]) // 2
    room = jnp.where((giver == order[0]) | (sink == order[0]) | (sizes[sink] == 0), 0, jnp.maximum(room, 0))
    passed = jax.random.randint(jax.random.fold_in(own, 4), (amount // 2,), 0, 1 << 20) % (room + 1)
    sizes = sizes.at[giver].add(-passed).at[sink].add(passed)
    members = jnp.searchsorted(jnp.cumsum(sizes), jnp.arange(rows * top), side="right").astype(jnp.int32)
    table = members.reshape(top, rows).T
    table = table[jax.random.permutation(jax.random.fold_in(own, 1), rows)]
    turn = jax.random.randint(jax.random.fold_in(own, 2), (rows, 1), 0, top)
    return jnp.take_along_axis(table, (jnp.arange(top)[None, :] + turn) % top, axis=1)


def shares(number_of, total, most, skew, full):
    loads = [(1 << 20) // math.isqrt(standing ** skew) + 1 for standing in range(1, number_of + 1)]
    largest = most if full else min(most, max(-(-total // number_of), total * loads[0] // sum(loads)))
    least = 1 if total - largest >= number_of - 1 else 0
    given, spare = [largest] + [least] * (number_of - 1), total - largest - least * (number_of - 1)
    while spare > 0:
        movable = [i for i in range(1, number_of) if given[i] < largest] or [i for i in range(1, number_of) if given[i] < most]
        pool, left = sum([loads[i] for i in movable]), spare
        for i in movable:
            more = min(most - given[i], max(1, left * loads[i] // pool), spare)
            given[i] = given[i] + more
            spare = spare - more
    return np.array(given)


def scatter_about(key, dims, width, limit, split=(), held_as=jnp.bfloat16):
    values = width * jax.random.normal(key, dims, jnp.float32)
    if split:
        values = values * shard_levels(key, dims, split, -0.22, 0.18)
    return jnp.clip(values, -limit, limit).astype(held_as)


def gaussian_with(key, shape, deviation, limit, shards, heavy, kind=jnp.bfloat16):
    result = deviation * jax.random.normal(key, shape, jnp.float32)
    if shards:
        result = result * shard_levels(key, shape, shards, -0.22, 0.18)
    return jnp.clip(spiked(result, jax.random.fold_in(key, 3), *heavy), -limit, limit).astype(kind)


def setup_inputs(seed: int = 0) -> dict:
    arg_keys = jax.random.split(jax.random.key(seed), 11)
    resid_in = scatter_about(arg_keys[0], (TOKENS, D), 1.0, 6.0, ((0, 32),))
    context = gaussian_with(arg_keys[1], (TOKENS, ATT), 1.0, 6.0, ((0, 2), (1, 16)), (1, 0, 16, 2.0))
    out_proj = scatter_about(arg_keys[2], (ATT, D), ATT ** -0.5, 0.125, ((0, 16),))
    norm_gain = jnp.clip(1.0 + 0.1 * jax.random.normal(arg_keys[3], (D,), jnp.float32), 0.5, 1.5)
    router = scatter_about(arg_keys[4], (D, EXPERTS), (16 * D) ** -0.5, 0.03125)
    routes_keys = jax.random.split(jax.random.fold_in(arg_keys[5], 1), TOKENS // TOK_DEV)
    routes_turns = jax.random.permutation(jax.random.fold_in(arg_keys[5], 3), TOKENS // TOK_DEV)
    routes = jax.vmap(lambda own, number: routed_block(jax.random.fold_in(arg_keys[5], 2), own, number, TOK_DEV, EXPERTS, TOP, MOST, 2))(routes_keys, routes_turns).reshape((TOKENS, TOP))
    w_gate = scatter_about(arg_keys[6], (D, EXPERTS * FF_E), D ** -0.5, 0.125, ((1, 32),))
    w_up = scatter_about(arg_keys[7], (D, EXPERTS * FF_E), D ** -0.5, 0.125, ((1, 32),))
    w_down = scatter_about(arg_keys[8], (EXPERTS * FF_E, D), (FF_E // 9) ** -0.5, 0.5, ((0, 32),))
    next_gain = jnp.clip(1.0 + 0.1 * jax.random.normal(arg_keys[9], (D,), jnp.float32), 0.5, 1.5)
    return {"resid_in": resid_in, "context": context, "out_proj": out_proj, "norm_gain": norm_gain, "router": router, "routes": routes, "w_gate": w_gate, "w_up": w_up, "w_down": w_down, "next_gain": next_gain}


def rms_norm(values, gain_row):
    widened = values.astype(jnp.float32)
    factor = lax.rsqrt(lax.optimization_barrier(jnp.mean(widened * widened, axis=-1, keepdims=True)) + 1e-06)
    return (widened * factor * gain_row).astype(jnp.bfloat16)

def reference(resid_in, context, out_proj, norm_gain, router, routes, w_gate, w_up, w_down, next_gain):
    attention = jnp.dot(context, out_proj, preferred_element_type=jnp.float32)
    hidden = (resid_in.astype(jnp.float32) + attention).astype(jnp.bfloat16)
    normed = rms_norm(hidden, norm_gain)
    logits = jnp.dot(normed, router, preferred_element_type=jnp.float32)
    picked = jnp.take_along_axis(logits, routes, axis=1)
    raised = jnp.exp(picked)
    route_weight = (raised / lax.optimization_barrier(jnp.sum(raised, axis=1, keepdims=True))).astype(jnp.bfloat16)
    flat_weight = route_weight.reshape(-1)
    flat_routes = routes.reshape(-1).astype(jnp.int32)
    sorted_order = jnp.argsort(flat_routes, stable=True).astype(jnp.int32)
    counts = lax.optimization_barrier(jnp.sum((flat_routes[:, None] == jnp.arange(EXPERTS, dtype=jnp.int32)[None, :]).astype(jnp.int32), axis=0)).astype(jnp.int32)
    starts = (jnp.cumsum(counts) - counts).astype(jnp.int32)
    window = MOST * (TOKENS // TOK_DEV)
    padded = jnp.concatenate([sorted_order, jnp.zeros((window,), jnp.int32)])
    block_size = min(UNITS, FF_E)
    block_count = FF_E // block_size

    def one_expert(expert_id, running):
        expert_id = jnp.asarray(expert_id).astype(jnp.int32)
        picked_index = lax.dynamic_slice_in_dim(padded, starts[expert_id].astype(jnp.int32), window)
        live_rows = jnp.arange(window, dtype=jnp.int32) < counts[expert_id]
        token_index = (picked_index // TOP).astype(jnp.int32)
        token_rows = normed[token_index]
        first = (expert_id * FF_E).astype(jnp.int32)
        gate_cols = lax.dynamic_slice_in_dim(w_gate, first, FF_E, 1)
        up_cols = lax.dynamic_slice_in_dim(w_up, first, FF_E, 1)
        down_rows = lax.dynamic_slice_in_dim(w_down, first, FF_E, 0)
        gate_h = jnp.dot(token_rows, gate_cols, preferred_element_type=jnp.float32)
        up_h = jnp.dot(token_rows, up_cols, preferred_element_type=jnp.float32)
        activated = (jax.nn.silu(gate_h) * up_h).astype(jnp.bfloat16)
        partials = jnp.einsum('rbf,bfd->rbd', activated.reshape(window, block_count, block_size).astype(jnp.float32), down_rows.reshape(block_count, block_size, D).astype(jnp.float32)).astype(jnp.bfloat16)
        weighted = jnp.where(live_rows, flat_weight[picked_index].astype(jnp.float32), jnp.float32(0.0))
        addition = lax.optimization_barrier(jnp.sum(partials.astype(jnp.float32), axis=1)) * weighted[:, None]
        return running.at[token_index].add(addition)
    expert_sum = lax.fori_loop(0, EXPERTS, one_expert, jnp.zeros((TOKENS, D), jnp.float32))
    resid_out = (hidden.astype(jnp.float32) + expert_sum).astype(jnp.bfloat16)
    next_normed = rms_norm(resid_out, next_gain)
    return (resid_out, next_normed)
```

```python
import jax
import jax.numpy as jnp
from jax import lax
from jax.sharding import PartitionSpec as P

FF_E = 1024
MOST = 10


def rms_norm(values, gain_row):
    widened = values.astype(jnp.float32)
    factor = lax.rsqrt(jnp.mean(widened * widened, axis=-1, keepdims=True) + 1e-06)
    return (widened * factor * gain_row).astype(jnp.bfloat16)


def project(context, out_proj, rep_count, ep_count):
    rep_at = lax.axis_index("rep")
    ep_at = lax.axis_index("ep")
    columns = out_proj.shape[1] // rep_count
    swap = [(i, (i + 1) % rep_count) for i in range(rep_count)]
    rows = context.shape[0] // ep_count
    blocks = context.reshape(ep_count, rows, context.shape[1])
    blocks = lax.all_to_all(blocks, "ep", split_axis=0, concat_axis=0, tiled=True)
    both = jnp.concatenate([blocks, lax.ppermute(blocks, "rep", swap)], axis=1)
    bits = list(range(ep_count.bit_length() - 1))[::-1]
    orders = [bits, bits[:-2] + bits[-2:][::-1]]
    held = lax.dynamic_slice_in_dim(out_proj, rep_at * columns, columns, 1)
    offsets = [[0], [0]]
    for step in range(len(bits)):
        perm = [
            (r * ep_count + e, r * ep_count + (e ^ (1 << orders[r][step])))
            for r in range(rep_count)
            for e in range(ep_count)
        ]
        held = jnp.concatenate([held, lax.ppermute(held, ("rep", "ep"), perm)], axis=0)
        offsets = [o + [v ^ (1 << orders[r][step]) for v in o] for r, o in enumerate(offsets)]
    places = jnp.bitwise_xor(jnp.array(offsets, jnp.int32)[rep_at], ep_at)
    ordered = jnp.take(both, places, axis=0)
    ordered = ordered.transpose(1, 0, 2).reshape(rep_count * rows, -1)
    product = jnp.dot(ordered, held, preferred_element_type=jnp.float32)
    mine = product[:rows]
    theirs = lax.ppermute(product[rows:], "rep", swap)
    return jnp.where(
        rep_at == 0,
        jnp.concatenate([mine, theirs], axis=1),
        jnp.concatenate([theirs, mine], axis=1),
    )


def body(resid_in, context, out_proj, norm_gain, router, routes, w_gate, w_up, w_down, next_gain):
    model_width = resid_in.shape[1]
    rep_count = lax.axis_size("rep")
    ep_count = lax.axis_size("ep")
    attention = project(context, out_proj, rep_count, ep_count)
    hidden = (resid_in.astype(jnp.float32) + attention).astype(jnp.bfloat16)
    normed = rms_norm(hidden, norm_gain)
    logits = jnp.dot(normed, router, preferred_element_type=jnp.float32)
    experts = router.shape[1]
    picked_mask = (
        routes[:, :, None] == jnp.arange(experts, dtype=jnp.int32)[None, None, :]
    ).astype(jnp.int32)
    picked = jnp.sum(picked_mask.astype(jnp.float32) * logits[:, None, :], axis=2)
    raised = jnp.exp(picked)
    route_weight = (raised / jnp.sum(raised, axis=1, keepdims=True)).astype(jnp.bfloat16)
    units = w_gate.shape[1]
    owners = max(FF_E // units, 1)
    per_device = max(units // FF_E, 1)
    block_size = min(units, FF_E)
    named_count = jnp.sum(picked_mask, axis=1)
    before = jnp.cumsum(named_count, axis=0) - named_count
    order_rank = jnp.sum(picked_mask * before[:, None, :], axis=2)
    owner_part = jnp.arange(owners, dtype=jnp.int32)
    target = (routes[:, :, None] * owners + owner_part[None, None, :]) // per_device
    local_expert = (routes % per_device)[:, :, None]
    slot_width = per_device * MOST
    slot_index = target * slot_width + local_expert * MOST + order_rank[:, :, None]
    slot_total = rep_count * ep_count * slot_width
    slot_hits = slot_index[None] == jnp.arange(slot_total, dtype=jnp.int32)[:, None, None, None]
    pair_hits = jnp.any(slot_hits, axis=3)
    placing = jnp.any(pair_hits, axis=2).astype(jnp.bfloat16)
    outgoing = jnp.dot(placing, normed, preferred_element_type=jnp.bfloat16)
    outgoing = outgoing.reshape(rep_count, ep_count, slot_width, model_width)
    arrived = lax.all_to_all(
        lax.all_to_all(outgoing, "rep", split_axis=0, concat_axis=0, tiled=True),
        "ep",
        split_axis=1,
        concat_axis=1,
        tiled=True,
    )
    slot_rows = arrived.reshape(rep_count * ep_count, per_device, MOST, model_width)
    outcomes = []
    for p in range(per_device):
        part = slice(p * block_size, (p + 1) * block_size)
        rows_p = slot_rows[:, p].reshape(-1, model_width)
        gate_h = jnp.dot(rows_p, w_gate[:, part], preferred_element_type=jnp.float32)
        up_h = jnp.dot(rows_p, w_up[:, part], preferred_element_type=jnp.float32)
        activated = (jax.nn.silu(gate_h) * up_h).astype(jnp.bfloat16)
        made = jnp.dot(activated, w_down[part], preferred_element_type=jnp.float32)
        outcomes.append(made.astype(jnp.bfloat16).reshape(-1, MOST, model_width))
    produced = jnp.stack(outcomes, axis=1)
    produced = produced.reshape(rep_count, ep_count, slot_width, model_width)
    returned = lax.all_to_all(
        lax.all_to_all(produced, "rep", split_axis=0, concat_axis=0, tiled=True),
        "ep",
        split_axis=1,
        concat_axis=1,
        tiled=True,
    )
    returned = returned.reshape(slot_total, model_width)
    weighing = jnp.einsum(
        "stk,tk->ts", pair_hits.astype(jnp.float32), route_weight.astype(jnp.float32)
    ).astype(jnp.bfloat16)
    expert_sum = jnp.dot(weighing, returned, preferred_element_type=jnp.float32)
    resid_out = (hidden.astype(jnp.float32) + expert_sum).astype(jnp.bfloat16)
    next_normed = rms_norm(resid_out, next_gain)
    return (resid_out, next_normed)


def solution(mesh):
    in_specs = (
        P(("rep", "ep"), None),
        P("rep", "ep"),
        P("ep", None),
        P(),
        P(),
        P(("rep", "ep"), None),
        P(None, ("rep", "ep")),
        P(None, ("rep", "ep")),
        P(("rep", "ep"), None),
        P(),
    )
    out_specs = (P(("rep", "ep"), None), P(("rep", "ep"), None))
    return jax.shard_map(body, mesh=mesh, in_specs=in_specs, out_specs=out_specs, check_vma=False)
```
